256 devices in a mesh: seq: 8 (over y, core), frame: 32 (over x, z).
Axes of the slice: x: 4, y: 4, z: 8, core: 2. Of those that a mesh axis runs over, the one named last changes fastest.
Arguments:
- queries: bfloat16 [32, 2048, 128], P('frame', 'seq'), may hold values from -8 to 8
- out_grad: bfloat16 [32, 2048, 128], P('frame', 'seq'), may hold values from -6 to 6
- keys: bfloat16 [4096, 32, 128], P('frame', 'seq'), may hold values from -8 to 8
- values: bfloat16 [4096, 32, 128], P('frame', 'seq'), may hold values from -6 to 6
- limits: int32 [2048], P('seq'), may hold values from 1 to 4096, as said below
- block_start: int32 [32], P('frame'), may hold values from 0 to 3968, as said below
Outputs:
- query_grad: float32 [32, 2048, 128], P('frame', 'seq')
- key_grad: float32 [4096, 32, 128], P('frame', 'seq')
- value_grad: float32 [4096, 32, 128], P('frame', 'seq')
The draws below stay inside these ranges and needn't reach their ends.
Inputs may be any that keep to these rules, and one draw needn't show every extreme that they name: `limits`: the last text row's limit is 4096. `block_start`: the entries are 128 times the block numbers 0 to 32 - 1, each once, in some order.
All inputs are finite; a program needn't handle non-finite values.
Results may differ from the reference program's by a relative error of at most 0.004.
The reference program's roundings to bfloat16 on the way (of `dscores` and `probs_low`) count: a program that leaves them out, or rounds other values in their place, can miss the bound.
Values may be sent and summed in bfloat16 or wider, within the bound.
A program may use at most 64 MiB of HBM per device.

```python
import jax
import jax.numpy as jnp
from jax import lax

H = 32
DH = 128
F_DEV = 128
TEXT = 2048
FRAMES = 4096
N_FRAME = 32


def common_axis(key):
    signs = jax.random.randint(key, (DH,), 0, 2)
    return signs.astype(jnp.float32) * 2.0 - 1.0


def draw_queries(key, part):
    axis_vec = common_axis(key)
    key = jax.random.fold_in(key, 11)
    drawn = jnp.clip(jax.random.normal(key, (H, TEXT, DH), jnp.float32), -6.0, 6.0)
    rows = jnp.arange(TEXT)
    strength = jnp.where(rows % 16 == 0, 4.0 + (rows // 16 % 5).astype(jnp.float32), 0.0)
    picked = strength[None, :, None] * axis_vec[None, None, :]
    full = jnp.where(strength[None, :, None] > 0.0, picked, drawn)
    return full.astype(jnp.bfloat16)


def draw_keys(key, part):
    axis_vec = common_axis(key)
    key = jax.random.fold_in(key, 12)
    drawn = jnp.clip(0.6 * jax.random.normal(key, (FRAMES, H, DH), jnp.float32), -3.0, 3.0)
    full = drawn + 5.0 * axis_vec[None, None, :]
    return full.astype(jnp.bfloat16)


def draw_limits(key, part):
    key = jax.random.fold_in(key, 13)
    rows = jnp.arange(TEXT, dtype=jnp.int32)
    base = 1 + rows * FRAMES // TEXT
    extra = jax.random.randint(key, (TEXT,), 0, F_DEV)
    bounded = jnp.minimum(base + extra, FRAMES)
    return jnp.where(rows == TEXT - 1, FRAMES, bounded).astype(jnp.int32)


def draw_block_start(key, part):
    key = jax.random.fold_in(key, 14)
    order = jax.random.permutation(key, N_FRAME)
    return (order * F_DEV).astype(jnp.int32)


def shard_levels(rng, dims, pieces, low, largest):
    level = 1.0
    for dim, parts in pieces:
        steps = jax.random.uniform(jax.random.fold_in(jax.random.fold_in(rng, 6), dim), (parts,), jnp.float32, low / len(pieces), largest / len(pieces))
        level = level * jnp.repeat(jnp.exp(steps), dims[dim] // parts).reshape((-1,) + (1,) * (len(dims) - 1 - dim))
    return level


def noise(stream_key, extent, deviation, bound, shards=(), kind=jnp.bfloat16):
    loudness = shard_levels(stream_key, extent, shards, -0.22, 0.18) if shards else 1.0
    values = jax.random.normal(stream_key, extent, jnp.float32) * deviation * loudness
    return jnp.minimum(jnp.maximum(values, -bound), bound).astype(kind)


def setup_inputs(seed: int = 0) -> dict:
    splits = jax.random.split(jax.random.key(seed), 7)
    return {
        "queries": draw_queries(jax.random.fold_in(splits[6], 71), 0),
        "out_grad": noise(splits[1], (H, TEXT, DH), 1.0, 6.0, ((0, 32), (1, 8))),
        "keys": draw_keys(jax.random.fold_in(splits[6], 71), 0),
        "values": noise(splits[3], (FRAMES, H, DH), 1.0, 6.0, ((0, 32), (1, 8))),
        "limits": draw_limits(jax.random.fold_in(splits[6], 71), 0),
        "block_start": draw_block_start(jax.random.fold_in(splits[6], 71), 0),
    }


NEG = -1e30


def reference(queries, out_grad, keys, values, limits, block_start):
    stamp = (block_start[:, None] + jnp.arange(F_DEV, dtype=jnp.int32)[None, :]).reshape(-1)
    visible = stamp[None, :] < limits[:, None]
    factor = DH ** -0.5

    def one_head(head):
        query = queries[head]
        grad = out_grad[head]
        key_rows = keys[:, head]
        value_rows = values[:, head]
        scores = jnp.dot(query, key_rows.T, preferred_element_type=jnp.float32) * factor
        scores = jnp.where(visible, scores, NEG)
        top = jnp.max(scores, axis=1)
        expo = jnp.where(visible, jnp.exp(scores - top[:, None]), jnp.float32(0.0))
        probs = expo / jnp.sum(expo, axis=1)[:, None]
        dprobs = jnp.dot(grad, value_rows.T, preferred_element_type=jnp.float32)
        delta = jnp.sum(probs * dprobs, axis=1)
        dscores = (probs * (dprobs - delta[:, None])).astype(jnp.bfloat16)
        probs_low = probs.astype(jnp.bfloat16)
        dq = jnp.dot(dscores, key_rows, preferred_element_type=jnp.float32) * factor
        dk = jnp.dot(dscores.T, query, preferred_element_type=jnp.float32) * factor
        dv = jnp.dot(probs_low.T, grad, preferred_element_type=jnp.float32)
        return dq, dk, dv

    dq, dk, dv = lax.map(one_head, jnp.arange(H, dtype=jnp.int32))
    return dq, jnp.transpose(dk, (1, 0, 2)), jnp.transpose(dv, (1, 0, 2))
```

```python
import functools

import jax
import jax.numpy as jnp
from jax import lax
from jax.experimental import pallas as pl
from jax.experimental.pallas import tpu as pltpu
from jax.sharding import PartitionSpec as P

MESH = pl.DeviceIdType.MESH
NEG = -1e30
FLOOR = -1e29
NT = (((1,), (1,)), ((), ()))


def kernel(
    nx, ny, nz,
    q_hbm, g_hbm, k_hbm, v_hbm, lim_hbm, bs_ref,
    out_in, dq_in,
    q_ref, g_ref, k_ref, v_ref, lim_ref,
    stage, kv_all, kt, q_all, g_all, lim_all, s_buf, dp_buf, m_blk, l_blk, d_blk, stat_all,
    part, part_in, out_send, dq_send, relay,
    in_ss, kv_ss, kv_rs, fw_ss, qg_ss, qg_rs, st_ss, st_rs, pt_ss, pt_rs, out_ss, out_rs,
    dy_ss, dy_rs, dx_ss, dx_rs,
):
    heads = nz // 2
    frames, _, width = k_ref.shape
    rows = q_ref.shape[0]
    factor = width ** (-0.5)
    seq, frame = lax.axis_index("seq"), lax.axis_index("frame")
    y, c = lax.div(seq, 2), lax.rem(seq, 2)
    x, z = lax.div(frame, nz), lax.rem(frame, nz)
    zc, zj, zp, zt = lax.div(z, heads), lax.rem(z, heads), lax.rem(z, 2), lax.div(z, 2)

    def at(px, py, pz, pc):
        return (py * 2 + pc, px * nz + pz)

    def near(k):
        if isinstance(k, int):
            step = (k + 1) // 2 if k % 2 else ny - k // 2
        else:
            step = jnp.where(lax.rem(k, 2) == 1, lax.div(k + 1, 2), ny - lax.div(k, 2))
        return lax.rem(y + step, ny)

    own_kv = jnp.logical_and(zc == c, zp == c)
    partner = at(x, y, z, 1 - c)
    kv_to = [at(x, y, heads * c + j, zp) for j in range(heads)]
    kv_from = [at(x, y, 2 * t + c, zc) for t in range(heads)]
    qg_to = [at(i, x, z, c) for i in range(nx)]
    qg_from = [at(y, i, z, c) for i in range(ny)]
    x_line = [at(i, y, z, c) for i in range(nx)]
    y_line = [at(x, i, z, c) for i in range(ny)]
    kv_to_self = [jnp.logical_and(own_kv, zj == j) for j in range(heads)]
    kv_from_self = [jnp.logical_and(own_kv, zt == t) for t in range(heads)]
    qg_to_self = [jnp.logical_and(x == y, x == i) for i in range(nx)]
    qg_from_self = [jnp.logical_and(x == y, y == i) for i in range(ny)]
    x_self = [x == i for i in range(nx)]
    y_self = [y == i for i in range(ny)]

    def remote(src, dst, ss, rs, to):
        return pltpu.make_async_remote_copy(
            src_ref=src, dst_ref=dst, send_sem=ss, recv_sem=rs, device_id=to, device_id_type=MESH
        )

    def send(src, dst, ss, rs, to, is_self):
        @pl.when(is_self)
        def _():
            pltpu.make_async_copy(src, dst, rs).start()

        @pl.when(jnp.logical_not(is_self))
        def _():
            remote(src, dst, ss, rs, to).start()

    def sent(src, dst, ss, rs, to, is_self):
        @pl.when(jnp.logical_not(is_self))
        def _():
            remote(src, dst, ss, rs, to).wait_send()

    def arrived(dst, rs):
        pltpu.make_async_copy(dst, dst, rs).wait()

    barrier = pltpu.get_barrier_semaphore()
    pl.semaphore_signal(barrier, inc=1, device_id=partner, device_id_type=MESH)
    count = jnp.int32(1)
    for to, is_self in zip(
        kv_from + kv_to + qg_from + qg_to + x_line + y_line,
        kv_from_self + kv_to_self + qg_from_self + qg_to_self + x_self + y_self,
    ):
        @pl.when(jnp.logical_not(is_self))
        def _(to=to):
            pl.semaphore_signal(barrier, inc=1, device_id=to, device_id_type=MESH)

        count = count + jnp.where(is_self, 0, 1)

    fetches = [
        pltpu.make_async_copy(src, dst, in_ss.at[n])
        for n, (src, dst) in enumerate(
            [(k_hbm, k_ref), (v_hbm, v_ref), (q_hbm, q_ref), (g_hbm, g_ref), (lim_hbm, lim_ref)]
        )
    ]
    for fetch in fetches:
        fetch.start()
    start_rows = jnp.full((16, width), bs_ref[0], jnp.int32).astype(jnp.float32)
    for j in range(heads):
        stage[j, 2 * frames :] = start_rows.astype(jnp.bfloat16)
    part[...] = jnp.zeros_like(part)
    fetches[0].wait()
    for j in range(heads):
        stage[j, 0:frames] = k_ref[:, j, :]
    fetches[1].wait()
    for j in range(heads):
        stage[j, frames : 2 * frames] = v_ref[:, j, :]
    for fetch in fetches[2:]:
        fetch.wait()

    pl.semaphore_wait(barrier, count)

    def kv_msg(j):
        return (stage.at[j], kv_all.at[z], kv_ss.at[j], kv_rs.at[z], kv_to[j], kv_to_self[j])

    def qg_msgs(i):
        return [
            (src, dst.at[y], qg_ss.at[n, i], qg_rs.at[n, y], qg_to[i], qg_to_self[i])
            for n, (src, dst) in enumerate([(q_ref, q_all), (g_ref, g_all), (lim_ref, lim_all)])
        ]

    def send_kv(n, _):
        j = lax.rem(zj + jnp.where(zc == c, heads - 1 - n + lax.div(heads, 2), n), heads)
        is_self = jnp.logical_and(own_kv, zj == j)
        send(
            stage.at[j], kv_all.at[z], kv_ss.at[j], kv_rs.at[z], at(x, y, heads * c + j, zp), is_self
        )
        return 0

    for i in range(nx):
        for msg in qg_msgs(i)[:2]:
            send(*msg)
    lax.fori_loop(0, heads, send_kv, 0)
    for i in range(nx):
        send(*qg_msgs(i)[2])

    place = lax.broadcasted_iota(jnp.int32, (frames, rows), 0).astype(jnp.float32)

    def block(b, i):
        here = pl.ds(pl.multiple_of(b * frames, frames), frames)
        k = kv_all[b, 0:frames]
        v = kv_all[b, frames : 2 * frames]
        start = kv_all[b, 2 * frames :].astype(jnp.float32)[0:1, :]
        limit = lim_all[i].astype(jnp.float32)
        room = jnp.concatenate(
            [limit[n : n + 1, :] - start[:, 0 : limit.shape[1]] for n in range(limit.shape[0])],
            axis=1,
        )
        raw = lax.dot_general(k, q_all[i], NT, preferred_element_type=jnp.float32)
        s = jnp.where(place < room, raw * factor, NEG)
        top = jnp.maximum(jnp.max(s, axis=0, keepdims=True), FLOOR)
        e = jnp.exp(s - top)
        dp = lax.dot_general(v, g_all[i], NT, preferred_element_type=jnp.float32)
        s_buf[i, here] = s
        dp_buf[i, here] = dp
        m_blk[i, pl.ds(b, 1)] = top
        l_blk[i, pl.ds(b, 1)] = jnp.sum(e, axis=0, keepdims=True)
        d_blk[i, pl.ds(b, 1)] = jnp.sum(e * dp, axis=0, keepdims=True)

    def st_msg(i, n):
        return (
            stat_all.at[x, i], stat_all.at[x, i], st_ss.at[n, i], st_rs.at[x, i], x_line[n],
        )

    def share_stats(i):
        m_all = m_blk[i]
        m = jnp.max(m_all, axis=0, keepdims=True)
        w = jnp.exp(m_all - m)
        stat_all[x, i, 0:1] = m
        stat_all[x, i, 1:2] = jnp.sum(w * l_blk[i], axis=0, keepdims=True)
        stat_all[x, i, 2:3] = jnp.sum(w * d_blk[i], axis=0, keepdims=True)
        stat_all[x, i, 3:4] = jnp.zeros_like(m)
        for n in range(nx):
            @pl.when(jnp.logical_not(x_self[n]))
            def _(n=n):
                remote(*st_msg(i, n)).start()

    def text_arrived(i):
        arrived(q_all.at[i], qg_rs.at[0, i])
        arrived(g_all.at[i], qg_rs.at[1, i])
        arrived(lim_all.at[i], qg_rs.at[2, i])

    base = z + lax.rem(z + c, 2)
    other = z + lax.rem(z + 1 - c, 2)

    def pair(n):
        m = lax.div(n + 1, 2) * 2
        step = jnp.where(lax.rem(n, 2) == 1, nz - m, m)
        return lax.rem(base + step, nz), lax.rem(other + step, nz)

    def take(b):
        arrived(kv_all.at[b], kv_rs.at[b])
        remote(kv_all.at[b], kv_all.at[b], fw_ss.at[b], kv_rs.at[b], partner).start()
        kt[b] = kv_all[b, 0:frames].T

    def take_passed(b):
        arrived(kv_all.at[b], kv_rs.at[b])
        kt[b] = kv_all[b, 0:frames].T

    def first_step(n, _):
        b, b2 = pair(n)
        take(b)
        block(b, y)
        take_passed(b2)
        block(b2, y)
        return 0

    def step(i, n, _):
        b, b2 = pair(n)
        block(b, i)
        block(b2, i)
        return 0

    def near_blocks(i):
        text_arrived(i)
        lax.fori_loop(0, heads - 1, functools.partial(step, i), 0)

    def far_blocks(k, _):
        i = near(k)
        step(i, jnp.int32(heads - 1), 0)
        share_stats(i)
        return 0

    text_arrived(y)
    lax.fori_loop(0, heads - 1, first_step, 0)
    near_blocks(near(1))
    last, last2 = pair(jnp.int32(heads - 1))
    take(last)
    if ny > 3:
        near_blocks(near(2))
    take_passed(last2)
    lax.fori_loop(0, max(ny - 1, 2), far_blocks, 0)
    if ny > 2:
        text_arrived(near(ny - 1))
        lax.fori_loop(0, heads, functools.partial(step, near(ny - 1)), 0)
        share_stats(near(ny - 1))

    def part_msg(t):
        return (part.at[t, 1 - c], part_in.at[t], pt_ss.at[t], pt_rs.at[t], partner)

    def out_msg(t):
        return (
            out_send.at[t], out_in.at[zj], out_ss.at[t], out_rs.at[zj],
            at(x, y, 2 * t + c, zc), jnp.logical_and(own_kv, zt == t),
        )

    def finish(t):
        arrived(part_in.at[t], pt_rs.at[t])
        out_send[t, 0] = ((part[t, c, 0] + part_in[t, 0]) * factor).astype(jnp.bfloat16)
        out_send[t, 1] = (part[t, c, 1] + part_in[t, 1]).astype(jnp.bfloat16)
        send(*out_msg(t))

    def dx_msg(a):
        return (relay.at[a], dq_in.at[x], dx_ss.at[a], dx_rs.at[x], at(a, y, z, c), x == a)

    def dy_msg(i):
        return (dq_send.at[i], relay.at[y], dy_ss.at[i], dy_rs.at[y], at(x, i, z, c))

    def far(t):
        return lax.rem(zt + [2, 1, 3, 0][t] if heads == 4 else zt + t, heads)

    def grads_chunk(i, last):
        for n in range(nx):
            @pl.when(jnp.logical_not(x_self[n]))
            def _(n=n):
                arrived(stat_all.at[n, i], st_rs.at[n, i])

        stats = [stat_all[n, i] for n in range(nx)]
        top = functools.reduce(jnp.maximum, [s[0:1] for s in stats])
        shares = [jnp.exp(s[0:1] - top) for s in stats]
        total = sum(w * s[1:2] for w, s in zip(shares, stats))
        delta = sum(w * s[2:3] for w, s in zip(shares, stats)) / total
        dqt = jnp.zeros((width, rows), jnp.float32)
        for n in range(heads):
            t = far(n)
            ds, low = [], []
            for h in range(2):
                b = 2 * t + h
                here = pl.ds(pl.multiple_of(b * frames, frames), frames)
                p = jnp.exp(s_buf[i, here] - top) / total
                ds.append((p * (dp_buf[i, here] - delta)).astype(jnp.bfloat16))
                low.append(p.astype(jnp.bfloat16))
            for h in range(2):
                part[t, h, 0] += jnp.dot(ds[h], q_all[i], preferred_element_type=jnp.float32)
                part[t, h, 1] += jnp.dot(low[h], g_all[i], preferred_element_type=jnp.float32)
            if last:
                remote(*part_msg(t)).start()
            dqt += jnp.dot(
                jnp.concatenate([kt[2 * t], kt[2 * t + 1]], axis=1),
                jnp.concatenate(ds, axis=0),
                preferred_element_type=jnp.float32,
            )
        return dqt.T * factor

    relay[y] = grads_chunk(y, False)
    send(*dx_msg(y))

    def middle(k, _):
        i = near(k)
        dq_send[i] = grads_chunk(i, False)
        remote(*dy_msg(i)).start()
        return 0

    lax.fori_loop(1, ny - 1, middle, 0)
    i = near(ny - 1)
    dq_send[i] = grads_chunk(i, True)
    remote(*dy_msg(i)).start()

    def pass_on(a):
        arrived(relay.at[a], dy_rs.at[a])
        send(*dx_msg(a))

    for n in range(heads):
        finish(far(n))
        if 1 <= n < ny - 1:
            pass_on(near(n))
    pass_on(near(ny - 1))

    for j in range(heads):
        arrived(out_in.at[j], out_rs.at[j])
    for i in range(nx):
        arrived(dq_in.at[i], dx_rs.at[i])

    for j in range(heads):
        sent(*kv_msg(j))
    for i in range(nx):
        for msg in qg_msgs(i):
            sent(*msg)

    def sent_step(n, _):
        b = pair(n)[0]
        remote(kv_all.at[b], kv_all.at[b], fw_ss.at[b], kv_rs.at[b], partner).wait_send()
        remote(*part_msg(n)).wait_send()
        sent(*out_msg(n))
        return 0

    def sent_chunk(i, _):
        for n in range(nx):
            @pl.when(jnp.logical_not(x_self[n]))
            def _(n=n):
                remote(*st_msg(i, n)).wait_send()

        @pl.when(i != y)
        def _():
            remote(*dy_msg(i)).wait_send()

        sent(*dx_msg(i))
        return 0

    lax.fori_loop(0, heads, sent_step, 0)
    lax.fori_loop(0, ny, sent_chunk, 0)


def place(out_in, dq_in, dq_hbm, dk_hbm, dv_hbm, dq, dk, dv, sems):
    dq[...] = functools.reduce(jnp.add, [dq_in[i] for i in range(dq_in.shape[0])])
    writes = [pltpu.make_async_copy(dq, dq_hbm, sems.at[0])]
    writes[0].start()
    for n, (buf, hbm) in enumerate([(dk, dk_hbm), (dv, dv_hbm)]):
        for j in range(out_in.shape[0]):
            buf[:, j, :] = out_in[j, n].astype(jnp.float32)
        writes.append(pltpu.make_async_copy(buf, hbm, sems.at[n + 1]))
        writes[-1].start()
    for write in writes:
        write.wait()


def body(nx, ny, nz, queries, out_grad, keys, values, limits, block_start):
    _, rows, width = queries.shape
    frames, heads, _ = keys.shape
    text, all_frames = ny * rows, nz * frames
    bf16, f32, dma, vmem = jnp.bfloat16, jnp.float32, pltpu.SemaphoreType.DMA, pltpu.VMEM
    lanes = min(rows, 128)
    limits = limits.reshape(rows // lanes, lanes)
    in_vmem = pl.BlockSpec(memory_space=pltpu.VMEM)
    in_hbm = pl.BlockSpec(memory_space=pltpu.HBM)
    out_in, dq_in = pl.pallas_call(
        functools.partial(kernel, nx, ny, nz),
        out_shape=(
            jax.ShapeDtypeStruct((heads, 2, frames, width), bf16),
            jax.ShapeDtypeStruct((nx, rows, width), f32),
        ),
        in_specs=[in_hbm] * 5 + [pl.BlockSpec(memory_space=pltpu.SMEM)],
        out_specs=[in_vmem] * 2,
        scratch_shapes=[
            vmem((rows, width), bf16),
            vmem((rows, width), bf16),
            vmem(keys.shape, bf16),
            vmem(keys.shape, bf16),
            vmem(limits.shape, jnp.int32),
            vmem((heads, 2 * frames + 16, width), bf16),
            vmem((nz, 2 * frames + 16, width), bf16),
            vmem((nz, width, frames), bf16),
            vmem((ny, rows, width), bf16),
            vmem((ny, rows, width), bf16),
            vmem((ny,) + limits.shape, jnp.int32),
            vmem((ny, all_frames, rows), f32),
            vmem((ny, all_frames, rows), f32),
            vmem((ny, nz, rows), f32),
            vmem((ny, nz, rows), f32),
            vmem((ny, nz, rows), f32),
            vmem((nx, ny, 4, rows), f32),
            vmem((heads, 2, 2, frames, width), f32),
            vmem((heads, 2, frames, width), f32),
            vmem((heads, 2, frames, width), bf16),
            vmem((ny, rows, width), f32),
            vmem((ny, rows, width), f32),
            dma((5,)),
            dma((heads,)), dma((nz,)), dma((nz,)),
            dma((3, nx)), dma((3, ny)),
            dma((nx, ny)), dma((nx, ny)),
            dma((heads,)), dma((heads,)),
            dma((heads,)), dma((heads,)),
            dma((ny,)), dma((ny,)),
            dma((ny,)), dma((nx,)),
        ],
        compiler_params=pltpu.CompilerParams(
            collective_id=0, has_side_effects=True, vmem_limit_bytes=60 * 1024 * 1024
        ),
    )(
        queries.reshape(rows, width), out_grad.reshape(rows, width), keys, values, limits,
        block_start,
    )
    dq, dk, dv = pl.pallas_call(
        place,
        out_shape=(
            jax.ShapeDtypeStruct((rows, width), f32),
            jax.ShapeDtypeStruct(keys.shape, f32),
            jax.ShapeDtypeStruct(values.shape, f32),
        ),
        in_specs=[in_vmem] * 2,
        out_specs=[in_hbm] * 3,
        scratch_shapes=[
            vmem((rows, width), f32), vmem(keys.shape, f32), vmem(values.shape, f32), dma((3,)),
        ],
    )(out_in, dq_in)
    return dq[None], dk, dv


def solution(mesh):
    ny = mesh.shape["seq"] // 2
    nx = ny
    nz = mesh.shape["frame"] // nx
    wide = P("frame", "seq", None)
    return jax.shard_map(
        functools.partial(body, nx, ny, nz),
        mesh=mesh,
        in_specs=(wide, wide, wide, wide, P("seq"), P("frame")),
        out_specs=(wide, wide, wide),
        check_vma=False,
    )
```

```python
import functools

import jax
import jax.numpy as jnp
from jax import lax
from jax.experimental import pallas as pl
from jax.experimental.pallas import tpu as pltpu
from jax.sharding import PartitionSpec as P

MESH = pl.DeviceIdType.MESH
NEG = -1e30
FLOOR = -1e29
NT = (((1,), (1,)), ((), ()))
TN = (((0,), (0,)), ((), ()))


def kernel(
    nx, ny, nz,
    q_hbm, g_hbm, k_hbm, v_hbm, lim_hbm, bs_ref,
    out_in, dq_in,
    q_ref, g_ref, k_ref, v_ref, lim_ref,
    stage, kv_all, kt, q_all, g_all, lim_all, s_buf, dp_buf, m_blk, l_blk, d_blk, stat_all,
    part, part_in, out_send, dq_send, relay,
    in_ss, kv_ss, kv_rs, fw_ss, qg_ss, qg_rs, st_ss, st_rs, pt_ss, pt_rs, out_ss, out_rs,
    dy_ss, dy_rs, dx_ss, dx_rs,
):
    heads = nz // 2
    frames, _, width = k_ref.shape
    rows = q_ref.shape[0]
    factor = width ** (-0.5)
    seq, frame = lax.axis_index("seq"), lax.axis_index("frame")
    y, c = lax.div(seq, 2), lax.rem(seq, 2)
    x, z = lax.div(frame, nz), lax.rem(frame, nz)
    zc, zj, zp, zt = lax.div(z, heads), lax.rem(z, heads), lax.rem(z, 2), lax.div(z, 2)

    def at(px, py, pz, pc):
        return (py * 2 + pc, px * nz + pz)

    def near(k):
        if isinstance(k, int):
            step = (k + 1) // 2 if k % 2 else ny - k // 2
        else:
            step = jnp.where(lax.rem(k, 2) == 1, lax.div(k + 1, 2), ny - lax.div(k, 2))
        return lax.rem(y + step, ny)

    own_kv = jnp.logical_and(zc == c, zp == c)
    partner = at(x, y, z, 1 - c)
    kv_to = [at(x, y, heads * c + j, zp) for j in range(heads)]
    kv_from = [at(x, y, 2 * t + c, zc) for t in range(heads)]
    qg_to = [at(i, x, z, c) for i in range(nx)]
    qg_from = [at(y, i, z, c) for i in range(ny)]
    x_line = [at(i, y, z, c) for i in range(nx)]
    y_line = [at(x, i, z, c) for i in range(ny)]
    kv_to_self = [jnp.logical_and(own_kv, zj == j) for j in range(heads)]
    kv_from_self = [jnp.logical_and(own_kv, zt == t) for t in range(heads)]
    qg_to_self = [jnp.logical_and(x == y, x == i) for i in range(nx)]
    qg_from_self = [jnp.logical_and(x == y, y == i) for i in range(ny)]
    x_self = [x == i for i in range(nx)]
    y_self = [y == i for i in range(ny)]

    def remote(src, dst, ss, rs, to):
        return pltpu.make_async_remote_copy(
            src_ref=src, dst_ref=dst, send_sem=ss, recv_sem=rs, device_id=to, device_id_type=MESH
        )

    def send(src, dst, ss, rs, to, is_self):
        @pl.when(is_self)
        def _():
            pltpu.make_async_copy(src, dst, rs).start()

        @pl.when(jnp.logical_not(is_self))
        def _():
            remote(src, dst, ss, rs, to).start()

    def sent(src, dst, ss, rs, to, is_self):
        @pl.when(jnp.logical_not(is_self))
        def _():
            remote(src, dst, ss, rs, to).wait_send()

    def arrived(dst, rs):
        pltpu.make_async_copy(dst, dst, rs).wait()

    barrier = pltpu.get_barrier_semaphore()
    pl.semaphore_signal(barrier, inc=1, device_id=partner, device_id_type=MESH)
    count = jnp.int32(1)
    for to, is_self in zip(
        kv_from + kv_to + qg_from + qg_to + x_line + y_line,
        kv_from_self + kv_to_self + qg_from_self + qg_to_self + x_self + y_self,
    ):
        @pl.when(jnp.logical_not(is_self))
        def _(to=to):
            pl.semaphore_signal(barrier, inc=1, device_id=to, device_id_type=MESH)

        count = count + jnp.where(is_self, 0, 1)

    fetches = [
        pltpu.make_async_copy(src, dst, in_ss.at[n])
        for n, (src, dst) in enumerate(
            [(k_hbm, k_ref), (v_hbm, v_ref), (q_hbm, q_ref), (g_hbm, g_ref), (lim_hbm, lim_ref)]
        )
    ]
    for fetch in fetches:
        fetch.start()
    start_rows = jnp.full((16, width), bs_ref[0], jnp.int32).astype(jnp.float32)
    for j in range(heads):
        stage[j, 2 * frames :] = start_rows.astype(jnp.bfloat16)
    part[...] = jnp.zeros_like(part)
    kt[:, width:] = jnp.ones_like(kt[:, width:])
    fetches[0].wait()
    for j in range(heads):
        stage[j, 0:frames] = k_ref[:, j, :]
    fetches[1].wait()
    for j in range(heads):
        stage[j, frames : 2 * frames] = v_ref[:, j, :]
    for fetch in fetches[2:]:
        fetch.wait()

    pl.semaphore_wait(barrier, count)

    def kv_msg(j):
        return (stage.at[j], kv_all.at[z], kv_ss.at[j], kv_rs.at[z], kv_to[j], kv_to_self[j])

    def qg_msgs(i):
        return [
            (src, dst.at[y], qg_ss.at[n, i], qg_rs.at[n, y], qg_to[i], qg_to_self[i])
            for n, (src, dst) in enumerate([(q_ref, q_all), (g_ref, g_all), (lim_ref, lim_all)])
        ]

    def send_kv(n, _):
        j = lax.rem(zj + jnp.where(zc == c, heads - 1 - n + lax.div(heads, 2), n), heads)
        is_self = jnp.logical_and(own_kv, zj == j)
        send(
            stage.at[j], kv_all.at[z], kv_ss.at[j], kv_rs.at[z], at(x, y, heads * c + j, zp), is_self
        )
        return 0

    for i in range(nx):
        for msg in qg_msgs(i)[:2]:
            send(*msg)
    lax.fori_loop(0, heads, send_kv, 0)
    for i in range(nx):
        send(*qg_msgs(i)[2])

    place = lax.broadcasted_iota(jnp.int32, (frames, rows), 0).astype(jnp.float32)

    def block(b, i):
        here = pl.ds(pl.multiple_of(b * frames, frames), frames)
        k = kv_all[b, 0:frames]
        v = kv_all[b, frames : 2 * frames]
        start = kv_all[b, 2 * frames :].astype(jnp.float32)[0:1, :]
        limit = lim_all[i].astype(jnp.float32)
        room = jnp.concatenate(
            [limit[n : n + 1, :] - start[:, 0 : limit.shape[1]] for n in range(limit.shape[0])],
            axis=1,
        )
        raw = lax.dot_general(k, q_all[i], NT, preferred_element_type=jnp.float32)
        s = jnp.where(place < room, raw * factor, NEG)
        top = jnp.maximum(jnp.max(s, axis=0, keepdims=True), FLOOR)
        e = jnp.exp(s - top)
        dp = lax.dot_general(v, g_all[i], NT, preferred_element_type=jnp.float32)
        s_buf[i, here] = s
        dp_buf[i, here] = dp
        m_blk[i, pl.ds(b, 1)] = top
        l_blk[i, pl.ds(b, 1)] = jnp.sum(e, axis=0, keepdims=True)
        d_blk[i, pl.ds(b, 1)] = jnp.sum(e * dp, axis=0, keepdims=True)

    def st_msg(i, n):
        return (
            stat_all.at[x, i], stat_all.at[x, i], st_ss.at[n, i], st_rs.at[x, i], x_line[n],
        )

    def share_stats(i):
        m_all = m_blk[i]
        m = jnp.max(m_all, axis=0, keepdims=True)
        w = jnp.exp(m_all - m)
        stat_all[x, i, 0:1] = m
        stat_all[x, i, 1:2] = jnp.sum(w * l_blk[i], axis=0, keepdims=True)
        stat_all[x, i, 2:3] = jnp.sum(w * d_blk[i], axis=0, keepdims=True)
        stat_all[x, i, 3:4] = jnp.zeros_like(m)
        for n in range(nx):
            @pl.when(jnp.logical_not(x_self[n]))
            def _(n=n):
                remote(*st_msg(i, n)).start()

    def text_arrived(i):
        arrived(q_all.at[i], qg_rs.at[0, i])
        arrived(g_all.at[i], qg_rs.at[1, i])
        arrived(lim_all.at[i], qg_rs.at[2, i])

    base = z + lax.rem(z + c, 2)
    other = z + lax.rem(z + 1 - c, 2)

    def pair(n):
        m = lax.div(n + 1, 2) * 2
        step = jnp.where(lax.rem(n, 2) == 1, nz - m, m)
        return lax.rem(base + step, nz), lax.rem(other + step, nz)

    def take(b):
        arrived(kv_all.at[b], kv_rs.at[b])
        remote(kv_all.at[b], kv_all.at[b], fw_ss.at[b], kv_rs.at[b], partner).start()
        kt[b, 0:width] = kv_all[b, 0:frames].T

    def take_passed(b):
        arrived(kv_all.at[b], kv_rs.at[b])
        kt[b, 0:width] = kv_all[b, 0:frames].T

    def first_step(n, _):
        b, b2 = pair(n)
        take(b)
        block(b, y)
        take_passed(b2)
        block(b2, y)
        return 0

    def step(i, n, _):
        b, b2 = pair(n)
        block(b, i)
        block(b2, i)
        return 0

    def near_blocks(i):
        text_arrived(i)
        lax.fori_loop(0, heads - 1, functools.partial(step, i), 0, unroll=True)

    def far_blocks(k, _):
        i = near(k)
        step(i, jnp.int32(heads - 1), 0)
        share_stats(i)
        return 0

    text_arrived(y)
    lax.fori_loop(0, heads - 1, first_step, 0)
    near_blocks(near(1))
    last, last2 = pair(jnp.int32(heads - 1))
    take(last)
    if ny > 3:
        near_blocks(near(2))
    take_passed(last2)
    lax.fori_loop(0, max(ny - 1, 2), far_blocks, 0)
    if ny > 2:
        text_arrived(near(ny - 1))
        lax.fori_loop(0, heads, functools.partial(step, near(ny - 1)), 0, unroll=True)
        share_stats(near(ny - 1))

    def part_msg(t):
        return (part.at[t, 1 - c], part_in.at[t], pt_ss.at[t], pt_rs.at[t], partner)

    def out_msg(t):
        return (
            out_send.at[t], out_in.at[zj], out_ss.at[t], out_rs.at[zj],
            at(x, y, 2 * t + c, zc), jnp.logical_and(own_kv, zt == t),
        )

    def finish(t):
        arrived(part_in.at[t], pt_rs.at[t])
        out_send[t, 0] = ((part[t, c, 0] + part_in[t, 0]) * factor).astype(jnp.bfloat16)
        out_send[t, 1] = (part[t, c, 1] + part_in[t, 1]).astype(jnp.bfloat16)
        send(*out_msg(t))

    def dx_msg(a):
        return (relay.at[a], dq_in.at[x], dx_ss.at[a], dx_rs.at[x], at(a, y, z, c), x == a)

    def dy_msg(i):
        return (dq_send.at[i], relay.at[y], dy_ss.at[i], dy_rs.at[y], at(x, i, z, c))

    def far(t):
        return lax.rem(zt + [2, 1, 3, 0][t] if heads == 4 else zt + t, heads)

    mean = sum(
        jnp.sum(kv_all[b, 0:frames].astype(jnp.float32), axis=0, keepdims=True) for b in range(nz)
    ) * (1.0 / (nz * frames))
    mean = mean.astype(jnp.bfloat16).astype(jnp.float32)
    mean_col = jnp.broadcast_to(mean, (width, width)).T
    spot = lax.broadcasted_iota(jnp.int32, (16, width), 0)

    def pack_dq(dst, terms):
        extra = jnp.where(spot == 3 * (rows // width), mean, 0.0)
        for n in range(rows // width):
            cols = slice(n * width, (n + 1) * width)
            whole = terms[width : width + 1, cols]
            dst[cols] = ((terms[0:width, cols] - mean_col * whole).T * factor).astype(jnp.bfloat16)
            rest = whole * factor
            for m in range(3):
                piece = rest.astype(jnp.bfloat16).astype(jnp.float32)
                extra = jnp.where(spot == 3 * n + m, piece, extra)
                rest = rest - piece
        dst[rows:] = extra.astype(jnp.bfloat16)

    def grads_chunk(i, last, dst):
        for n in range(nx):
            @pl.when(jnp.logical_not(x_self[n]))
            def _(n=n):
                arrived(stat_all.at[n, i], st_rs.at[n, i])

        stats = [stat_all[n, i] for n in range(nx)]
        top = functools.reduce(jnp.maximum, [s[0:1] for s in stats])
        shares = [jnp.exp(s[0:1] - top) for s in stats]
        total = sum(w * s[1:2] for w, s in zip(shares, stats))
        delta = sum(w * s[2:3] for w, s in zip(shares, stats)) / total
        dqt = jnp.zeros((width + 16, rows), jnp.float32)
        for n in range(heads):
            t = far(n)
            ds, low = [], []
            for h in range(2):
                b = 2 * t + h
                here = pl.ds(pl.multiple_of(b * frames, frames), frames)
                p = jnp.exp(s_buf[i, here] - top) / total
                ds.append((p * (dp_buf[i, here] - delta)).astype(jnp.bfloat16))
                low.append(p.astype(jnp.bfloat16))
            for h in range(2):
                part[t, h, 0] += jnp.dot(ds[h], q_all[i], preferred_element_type=jnp.float32)
                part[t, h, 1] += jnp.dot(low[h], g_all[i], preferred_element_type=jnp.float32)
            if last:
                remote(*part_msg(t)).start()
            dqt += jnp.dot(
                jnp.concatenate([kt[2 * t], kt[2 * t + 1]], axis=1),
                jnp.concatenate(ds, axis=0),
                preferred_element_type=jnp.float32,
            )
        pack_dq(dst, dqt)

    grads_chunk(y, False, relay.at[y])
    send(*dx_msg(y))

    def middle(k, _):
        i = near(k)
        grads_chunk(i, False, dq_send.at[i])
        remote(*dy_msg(i)).start()
        return 0

    lax.fori_loop(1, ny - 1, middle, 0)
    i = near(ny - 1)
    grads_chunk(i, True, dq_send.at[i])
    remote(*dy_msg(i)).start()

    def pass_on(a):
        arrived(relay.at[a], dy_rs.at[a])
        send(*dx_msg(a))

    for n in range(heads):
        finish(far(n))
        if 1 <= n < ny - 1:
            pass_on(near(n))
    pass_on(near(ny - 1))

    for j in range(heads):
        arrived(out_in.at[j], out_rs.at[j])
    for i in range(nx):
        arrived(dq_in.at[i], dx_rs.at[i])

    for j in range(heads):
        sent(*kv_msg(j))
    for i in range(nx):
        for msg in qg_msgs(i):
            sent(*msg)

    def sent_step(n, _):
        b = pair(n)[0]
        remote(kv_all.at[b], kv_all.at[b], fw_ss.at[b], kv_rs.at[b], partner).wait_send()
        remote(*part_msg(n)).wait_send()
        sent(*out_msg(n))
        return 0

    def sent_chunk(i, _):
        for n in range(nx):
            @pl.when(jnp.logical_not(x_self[n]))
            def _(n=n):
                remote(*st_msg(i, n)).wait_send()

        @pl.when(i != y)
        def _():
            remote(*dy_msg(i)).wait_send()

        sent(*dx_msg(i))
        return 0

    lax.fori_loop(0, heads, sent_step, 0)
    lax.fori_loop(0, ny, sent_chunk, 0)


def place(out_in, dq_in, dq_hbm, dk_hbm, dv_hbm, dq, dk, dv, sems):
    rows, width = dq.shape
    halves = rows // width
    parts = range(dq_in.shape[0])
    extra = [dq_in[i, rows:].astype(jnp.float32) for i in parts]
    means = [jnp.broadcast_to(e[3 * halves : 3 * halves + 1], e.shape) for e in extra]
    means = jnp.concatenate(means, axis=0).astype(jnp.bfloat16)
    spot = lax.broadcasted_iota(jnp.int32, extra[0].shape, 0)
    for n in range(halves):
        here = slice(n * width, (n + 1) * width)
        sums = [jnp.where(lax.div(spot, 3) == n, e, 0.0) for e in extra]
        sums = jnp.concatenate(sums, axis=0).astype(jnp.bfloat16)
        common = lax.dot_general(sums, means, TN, preferred_element_type=jnp.float32)
        dq[here] = functools.reduce(
            jnp.add, [dq_in[i, here].astype(jnp.float32) for i in parts], common
        )
    writes = [pltpu.make_async_copy(dq, dq_hbm, sems.at[0])]
    writes[0].start()
    for n, (buf, hbm) in enumerate([(dk, dk_hbm), (dv, dv_hbm)]):
        for j in range(out_in.shape[0]):
            buf[:, j, :] = out_in[j, n].astype(jnp.float32)
        writes.append(pltpu.make_async_copy(buf, hbm, sems.at[n + 1]))
        writes[-1].start()
    for write in writes:
        write.wait()


def body(nx, ny, nz, queries, out_grad, keys, values, limits, block_start):
    _, rows, width = queries.shape
    frames, heads, _ = keys.shape
    text, all_frames = ny * rows, nz * frames
    bf16, f32, dma, vmem = jnp.bfloat16, jnp.float32, pltpu.SemaphoreType.DMA, pltpu.VMEM
    lanes = min(rows, 128)
    limits = limits.reshape(rows // lanes, lanes)
    in_vmem = pl.BlockSpec(memory_space=pltpu.VMEM)
    in_hbm = pl.BlockSpec(memory_space=pltpu.HBM)
    out_in, dq_in = pl.pallas_call(
        functools.partial(kernel, nx, ny, nz),
        out_shape=(
            jax.ShapeDtypeStruct((heads, 2, frames, width), bf16),
            jax.ShapeDtypeStruct((nx, rows + 16, width), bf16),
        ),
        in_specs=[in_hbm] * 5 + [pl.BlockSpec(memory_space=pltpu.SMEM)],
        out_specs=[in_vmem] * 2,
        scratch_shapes=[
            vmem((rows, width), bf16),
            vmem((rows, width), bf16),
            vmem(keys.shape, bf16),
            vmem(keys.shape, bf16),
            vmem(limits.shape, jnp.int32),
            vmem((heads, 2 * frames + 16, width), bf16),
            vmem((nz, 2 * frames + 16, width), bf16),
            vmem((nz, width + 16, frames), bf16),
            vmem((ny, rows, width), bf16),
            vmem((ny, rows, width), bf16),
            vmem((ny,) + limits.shape, jnp.int32),
            vmem((ny, all_frames, rows), f32),
            vmem((ny, all_frames, rows), f32),
            vmem((ny, nz, rows), f32),
            vmem((ny, nz, rows), f32),
            vmem((ny, nz, rows), f32),
            vmem((nx, ny, 4, rows), f32),
            vmem((heads, 2, 2, frames, width), f32),
            vmem((heads, 2, frames, width), f32),
            vmem((heads, 2, frames, width), bf16),
            vmem((ny, rows + 16, width), bf16),
            vmem((ny, rows + 16, width), bf16),
            dma((5,)),
            dma((heads,)), dma((nz,)), dma((nz,)),
            dma((3, nx)), dma((3, ny)),
            dma((nx, ny)), dma((nx, ny)),
            dma((heads,)), dma((heads,)),
            dma((heads,)), dma((heads,)),
            dma((ny,)), dma((ny,)),
            dma((ny,)), dma((nx,)),
        ],
        compiler_params=pltpu.CompilerParams(
            collective_id=0, has_side_effects=True, vmem_limit_bytes=60 * 1024 * 1024
        ),
    )(
        queries.reshape(rows, width), out_grad.reshape(rows, width), keys, values, limits,
        block_start,
    )
    dq, dk, dv = pl.pallas_call(
        place,
        out_shape=(
            jax.ShapeDtypeStruct((rows, width), f32),
            jax.ShapeDtypeStruct(keys.shape, f32),
            jax.ShapeDtypeStruct(values.shape, f32),
        ),
        in_specs=[in_vmem] * 2,
        out_specs=[in_hbm] * 3,
        scratch_shapes=[
            vmem((rows, width), f32), vmem(keys.shape, f32), vmem(values.shape, f32), dma((3,)),
        ],
    )(out_in, dq_in)
    return dq[None], dk, dv


def solution(mesh):
    ny = mesh.shape["seq"] // 2
    nx = ny
    nz = mesh.shape["frame"] // nx
    wide = P("frame", "seq", None)
    return jax.shard_map(
        functools.partial(body, nx, ny, nz),
        mesh=mesh,
        in_specs=(wide, wide, wide, wide, P("seq"), P("frame")),
        out_specs=(wide, wide, wide),
        check_vma=False,
    )
```
